128 devices in a mesh: vrow: 8 (over z, core), vcol: 16 (over x, y).
Axes of the slice: x: 4, y: 4, z: 4, core: 2. Of those that a mesh axis runs over, the one named last changes fastest.
Arguments:
- pair_amps: bfloat16 [768, 32768], P('vrow', 'vcol'), may hold values from -6 to 6
- integrals: bfloat16 [8, 16, 512, 128, 128], P('vrow', 'vcol'), may hold values from -0.046875 to 0.046875
- block_index: int32 [8, 16, 512], P('vrow', 'vcol'), may hold values from 0 to 511, as said below
- block_count: int32 [8, 16], P('vrow', 'vcol'), may hold values from 64 to 512, as said below
Outputs:
- ladder: bfloat16 [768, 32768], P('vcol', 'vrow')
The draws below stay inside these ranges and needn't reach their ends.
Inputs may be any that keep to these rules, and one draw needn't show every extreme that they name: Within one device group (g, h) the entries of block_index are distinct, a permutation of all 512 tile pairs. `block_count`: some device group holds all 512 slots live.
All inputs are finite; a program needn't handle non-finite values.
Results may differ from the reference program's by a relative error of at most 0.001.
Values may be sent and summed in bfloat16 or wider, within the bound.
A program may use at most 128 MiB of HBM per device.

```python
import jax
import jax.numpy as jnp
from jax import lax

VIRTUAL_PAIRS = 128
PAIRS = 768
ABT_DEV = 32
CD_PAIR_TILES = 16
SLOTS_PER_UNIT = 512
CD_TILES = 256
N_VROW = 8
N_VCOL = 16


def shuffle_one(subkey):
    return jax.random.permutation(subkey, ABT_DEV * CD_PAIR_TILES)


def draw_block_index(key, part):
    key = jax.random.fold_in(key, 11)
    subkeys = jax.random.split(key, N_VROW * N_VCOL)
    shuffled = jax.vmap(shuffle_one)(subkeys)
    return shuffled.reshape(N_VROW, N_VCOL, ABT_DEV * CD_PAIR_TILES).astype(jnp.int32)


def draw_block_count(key, part):
    key = jax.random.fold_in(key, 23)
    first_key, second_key = jax.random.split(key)
    smallest_count = max(SLOTS_PER_UNIT // 8, 1)
    count_range = jax.random.randint(first_key, (N_VROW * N_VCOL,), 0, 64)
    count_values = smallest_count + (SLOTS_PER_UNIT - smallest_count) * count_range * count_range // 3969
    largest_count = jax.random.randint(second_key, (), 0, N_VROW * N_VCOL)
    count_values = jnp.where(jnp.arange(N_VROW * N_VCOL) == largest_count, SLOTS_PER_UNIT, count_values)
    return count_values.reshape(N_VROW, N_VCOL).astype(jnp.int32)


def strengthened(result, key, source, target, parts, factor):
    owner, partner = [(jnp.arange(result.shape[axis_at]) // (result.shape[axis_at] // parts)).reshape([-1 if axis == axis_at else 1 for axis in range(result.ndim)]) for axis_at in (source, target)]
    chosen = jax.random.permutation(key, parts)[partner]
    strong = (owner == chosen) | (owner == (partner + parts // 2) % parts)
    return jnp.where(strong, factor * result, result)


def shard_levels(stream_key, shape, pieces, least, high):
    gain = 1.0
    for dim, blocks in pieces:
        draws = jax.random.uniform(jax.random.fold_in(jax.random.fold_in(stream_key, 6), dim), (blocks,), jnp.float32, least / len(pieces), high / len(pieces))
        gain = gain * jnp.repeat(jnp.exp(draws), shape[dim] // blocks).reshape((-1,) + (1,) * (len(shape) - 1 - dim))
    return gain


def bell_draw(key, dims, scale, bound, cuts=(), kind=jnp.bfloat16):
    values = scale * jax.random.normal(key, dims, jnp.float32)
    if cuts:
        values = values * shard_levels(key, dims, cuts, -0.22, 0.18)
    return jnp.clip(values, -bound, bound).astype(kind)


def noise_with(key, shape, scale, reach, cuts, heavy, kind=jnp.bfloat16):
    result = scale * jax.random.normal(key, shape, jnp.float32)
    if cuts:
        result = result * shard_levels(key, shape, cuts, -0.22, 0.18)
    return jnp.clip(strengthened(result, jax.random.fold_in(key, 3), *heavy), -reach, reach).astype(kind)


def setup_inputs(seed: int = 0) -> dict:
    splits = jax.random.split(jax.random.key(seed), 5)
    return {
        "pair_amps": noise_with(splits[0], (PAIRS, CD_TILES * VIRTUAL_PAIRS), 1.0, 6.0, ((0, 8), (1, 16)), (1, 0, 16, 2.0)),
        "integrals": bell_draw(splits[1], (N_VROW, N_VCOL, SLOTS_PER_UNIT, VIRTUAL_PAIRS, VIRTUAL_PAIRS), (VIRTUAL_PAIRS * CD_PAIR_TILES * N_VCOL // 2) ** -0.5, 0.046875, ((0, 8), (1, 16))),
        "block_index": draw_block_index(jax.random.fold_in(splits[4], 71), 0),
        "block_count": draw_block_count(jax.random.fold_in(splits[4], 71), 0),
    }


def reference(pair_amps, integrals, block_index, block_count):
    tile_size = integrals.shape[-1]
    slot_total = integrals.shape[2]
    pair_total = pair_amps.shape[0]
    amp_tiles = pair_amps.reshape(pair_total, N_VCOL, CD_PAIR_TILES, tile_size)
    slot_ids = jnp.arange(slot_total, dtype=jnp.int32)

    def row_block(row_group):
        def add_column(totals, col_group):
            slot_index = block_index[row_group, col_group]
            keep_mask = slot_ids < block_count[row_group, col_group]
            weights = jnp.where(keep_mask[:, None, None], integrals[row_group, col_group], jnp.zeros((), jnp.bfloat16))
            picked = jnp.take(amp_tiles[:, col_group], slot_index % CD_PAIR_TILES, axis=1)
            products = jnp.einsum("psc,sca->psa", picked.astype(jnp.float32), weights.astype(jnp.float32))
            totals = totals.at[:, slot_index // CD_PAIR_TILES, :].add(products)
            return totals, None

        start = jnp.zeros((pair_total, ABT_DEV, tile_size), jnp.float32)
        totals, unused = lax.scan(add_column, start, jnp.arange(N_VCOL, dtype=jnp.int32))
        return totals

    blocks = lax.map(row_block, jnp.arange(N_VROW, dtype=jnp.int32))
    residual = jnp.transpose(blocks, (1, 0, 2, 3)).reshape(pair_total, N_VROW * ABT_DEV * tile_size)
    mirrored = jnp.roll(residual, pair_total // 2, axis=0)
    return (residual - mirrored).astype(jnp.bfloat16)
```

```python
import jax
import jax.numpy as jnp
from jax import lax
from jax.experimental import pallas as pl
from jax.experimental.pallas import tpu as pltpu
from jax.sharding import PartitionSpec as P

MESH = pl.DeviceIdType.MESH
F32 = jnp.float32
TILE = 128
SLOTS = 512
CD = 16
DEPTH = CD * TILE
PASSES = 3
COLS = 512
UNITS = 24
PER_PASS = 8
LEVELS = 32766.0
PARTS = 16


def dims_of(rotation):
    return [(rotation + k) % 4 for k in range(4)]


def mask_of(position, dims):
    mask = 0
    for k in range(4):
        mask |= ((position >> (3 - k)) & 1) << dims[k]
    return mask


def kernel(
    inv, amps, w_hbm, out, wv, a, d, s0, s1, s2, s3, r0, r1, r2, r3, held,
    wsem, asem, gsend, grecv, ssend, srecv,
):
    vrow, vcol = lax.axis_index("vrow"), lax.axis_index("vcol")
    z, core = vrow // 2, vrow % 2
    x, y = vcol // 4, vcol % 4
    sent, got = [s0, s1, s2, s3], [r0, r1, r2, r3]

    per = SLOTS // PARTS

    def load_part(c):
        part = pl.ds(c * per, per)
        return pltpu.make_async_copy(w_hbm.at[part], wv.at[part], wsem.at[c])

    def load_rows(s, i):
        return pltpu.make_async_copy(
            amps.at[pl.ds(48 * i + 16 * s, 16)],
            a.at[s, pl.ds(32 * vrow + 16 * i, 16)],
            asem.at[2 * s + i],
        )

    for s in range(PASSES):
        for i in range(2):
            load_rows(s, i).start()
    for c in range(PARTS):
        load_part(c).start()

    above, below = (vrow + 2) % 8, (vrow + 6) % 8
    sibling = 2 * z + 1 - core
    partner = [
        (x + 1 - 2 * (x % 2)) * 4 + y,
        x * 4 + (y + 1 - 2 * (y % 2)),
        (3 - x) * 4 + y,
        x * 4 + (3 - y),
    ]
    opposite = ((x + 2) % 4) * 4 + y

    barrier = pltpu.get_barrier_semaphore()
    peers = [(above, vcol), (below, vcol), (sibling, vcol)]
    peers += [(vrow, p) for p in partner] + [(vrow, opposite)]
    for peer in peers:
        pl.semaphore_signal(barrier, inc=1, device_id=peer, device_id_type=MESH)
    wv[SLOTS] = jnp.zeros((TILE, TILE), jnp.bfloat16)
    for s in range(PASSES):
        for i in range(2):
            load_rows(s, i).wait()
    pl.semaphore_wait(barrier, len(peers))

    def piece(s, first, rows, target, kind):
        ref = a.at[s, pl.ds(pl.multiple_of(first, 16), rows)]
        return pltpu.make_async_remote_copy(
            src_ref=ref, dst_ref=ref,
            send_sem=gsend.at[s, kind], recv_sem=grecv.at[s, kind],
            device_id=(target, vcol), device_id_type=MESH,
        )

    own, low, high, far = 32 * vrow, 32 * below, 32 * above, 32 * ((vrow + 4) % 8)
    near = 32 * sibling

    def gather_copy(s, kind):
        first, rows, target = [
            (own, 32, above), (own, 32, below), (own, 32, sibling),
            (low, 16, above), (low, 32, sibling),
            (high + 16, 16, below), (high, 32, sibling),
            (far, 32, sibling),
        ][kind]
        return piece(s, first, rows, target, kind)

    def arrived(s, kind):
        first, rows = [
            (low, 32), (high, 32), (near, 32), (far, 16),
            (32 * ((sibling + 6) % 8), 32), (far + 16, 16),
            (32 * ((sibling + 2) % 8), 32), (32 * ((sibling + 4) % 8), 32),
        ][kind]
        piece(s, first, rows, sibling, kind).wait_recv()

    def gather_start(s):
        for kind in (0, 1, 2):
            gather_copy(s, kind).start()

    def gather_forward(s):
        arrived(s, 0)
        gather_copy(s, 3).start()
        gather_copy(s, 4).start()
        arrived(s, 1)
        gather_copy(s, 5).start()
        gather_copy(s, 6).start()

    def gather_last(s):
        arrived(s, 3)
        arrived(s, 5)
        gather_copy(s, 7).start()

    def gather_end(s):
        for kind in (2, 4, 6, 7):
            arrived(s, kind)

    xa, xb = ((x + 1) // 2) % 2, x // 2
    ya, yb = ((y + 1) // 2) % 2, y // 2
    place = []
    for m in range(16):
        ta, tya = (xa + (m & 1)) % 2, (ya + ((m >> 1) & 1)) % 2
        tb, tyb = (xb + ((m >> 2) & 1)) % 2, (yb + ((m >> 3) & 1)) % 2
        group = 4 * ((ta + tb) % 2) + 2 * tyb + (tya + tyb) % 2
        place.append((pl.multiple_of(16 * group, 16), pl.multiple_of(256 * tb, 256)))

    def share(u, position, dims):
        row, col = place[mask_of(position, dims)]
        return d.at[u, pl.ds(row, 16), pl.ds(col, 256)]

    def exchange(u, k, dims):
        return pltpu.make_async_remote_copy(
            src_ref=sent[k].at[u], dst_ref=got[k].at[u],
            send_sem=ssend.at[u, k], recv_sem=srecv.at[u, k],
            device_id=(vrow, partner[dims[k]]), device_id_type=MESH,
        )

    def pack(u, k, values):
        most = jnp.abs(values[0])
        for value in values[1:]:
            most = jnp.maximum(most, jnp.abs(value))
        most = jnp.maximum(jnp.max(most, axis=0, keepdims=True), 1e-30)
        code = jnp.ceil(jnp.log(most) * 256.0)
        factor = jnp.exp(code * (-1.0 / 256.0)) * LEVELS
        for n, value in enumerate(values):
            q = jnp.round(value * factor).astype(jnp.int32)
            sent[k][u, 16 * n : 16 * n + 16] = q.astype(jnp.int16)
        n = len(values)
        wide = jnp.broadcast_to(code, (16, 256)).astype(jnp.int32)
        sent[k][u, 16 * n : 16 * n + 16] = wide.astype(jnp.int16)

    def unpack(u, k, n):
        count = 8 >> k
        code = got[k][u, 16 * count : 16 * count + 16].astype(jnp.int32).astype(F32)
        factor = jnp.exp(code * (1.0 / 256.0)) * (1.0 / LEVELS)
        q = got[k][u, 16 * n : 16 * n + 16].astype(jnp.int32).astype(F32)
        return q * factor

    def multiply(u):
        s, j = u // PER_PASS, u % PER_PASS
        right = []
        for t in range(COLS // TILE):
            blocks = [wv[inv[(j * 4 + t) * CD + k]] for k in range(CD)]
            right.append(jnp.concatenate(blocks, 0))
        right = jnp.concatenate(right, 1)
        plus = jnp.dot(a[s, 0:128], right, preferred_element_type=F32)
        minus = jnp.dot(a[s, 128:256], right, preferred_element_type=F32)
        d[u] = plus - minus

    def first_pack(u, dims):
        pack(u, 0, [share(u, p, dims)[...] for p in range(8, 16)])

    def middle(u, k, dims):
        count = 16 >> k
        half = count // 2
        pack(u, k, [share(u, p, dims)[...] + unpack(u, k - 1, p) for p in range(half, count)])
        for p in range(half):
            ref = share(u, p, dims)
            ref[...] = ref[...] + unpack(u, k - 1, p)

    def out_ref(u):
        s, j = u // PER_PASS, u % PER_PASS
        col = pl.multiple_of(COLS * j + 256 * xb, 256)
        return held.at[pl.ds(pl.multiple_of(16 * s, 16), 16), pl.ds(col, 256)]

    def last(u, dims):
        total = share(u, 0, dims)[...] + unpack(u, 3, 0)
        out_ref(u)[...] = total.astype(jnp.bfloat16)

    def deliver(u):
        return pltpu.make_async_remote_copy(
            src_ref=out_ref(u), dst_ref=out_ref(u),
            send_sem=ssend.at[u, 4], recv_sem=srecv.at[u, 4],
            device_id=(vrow, opposite), device_id_type=MESH,
        )

    gather_start(0)
    gather_forward(0)
    gather_last(0)
    for c in range(PARTS):
        load_part(c).wait()

    rounds = UNITS // 4

    def turn(it, unused):
        @pl.when((it % 2 == 0) & (it < rounds))
        def _():
            gather_end(it // 2)

            @pl.when(it < rounds - 2)
            def _():
                gather_start(it // 2 + 1)

        @pl.when((it % 2 == 1) & (it < rounds - 2))
        def _():
            gather_forward(it // 2 + 1)

        for r in range(4):
            dims = dims_of(r)
            for k in (4, 3, 2, 1):
                @pl.when((it >= k) & (it < rounds + k))
                def _():
                    u = (it - k) * 4 + r
                    exchange(u, k - 1, dims).wait_recv()
                    if k == 4:
                        last(u, dims)
                        deliver(u).start()
                    else:
                        middle(u, k, dims)
                        exchange(u, k, dims).start()

            @pl.when(it < rounds)
            def _():
                u = it * 4 + r
                multiply(u)
                first_pack(u, dims)
                exchange(u, 0, dims).start()

            if r == 2:
                @pl.when((it % 2 == 1) & (it < rounds - 2))
                def _():
                    gather_last(it // 2 + 1)
        return unused

    lax.fori_loop(0, rounds + 4, turn, 0)

    def finish(u, unused):
        for k in range(4):
            exchange(u, k, [0, 1, 2, 3]).wait_send()
        deliver(u).wait_send()
        s, j = u // PER_PASS, u % PER_PASS
        col = pl.multiple_of(COLS * j + 256 * (1 - xb), 256)
        ref = held.at[pl.ds(pl.multiple_of(16 * s, 16), 16), pl.ds(col, 256)]
        pltpu.make_async_remote_copy(
            src_ref=ref, dst_ref=ref,
            send_sem=ssend.at[u, 4], recv_sem=srecv.at[u, 4],
            device_id=(vrow, opposite), device_id_type=MESH,
        ).wait_recv()
        return unused

    lax.fori_loop(0, UNITS, finish, 0)
    for s in range(PASSES):
        for kind in range(8):
            gather_copy(s, kind).wait_send()

    sign = (1 - 2 * xb).astype(jnp.bfloat16)
    out[...] = held[...] * sign


def per_device(pair_amps, integrals, block_index, block_count):
    slot_ids = jnp.arange(SLOTS, dtype=jnp.int32)
    index = jnp.where(slot_ids < block_count[0, 0], block_index[0, 0], SLOTS)
    hit = index[None, :] == slot_ids[:, None]
    inverse = SLOTS + jnp.sum(jnp.where(hit, slot_ids[None, :] - SLOTS, 0), axis=1)
    messages = [pltpu.VMEM((UNITS, (128 >> k) + 16, 256), jnp.int16) for k in range(4)]
    return pl.pallas_call(
        kernel,
        out_shape=jax.ShapeDtypeStruct((48, 4096), jnp.bfloat16),
        in_specs=[
            pl.BlockSpec(memory_space=pltpu.SMEM),
            pl.BlockSpec(memory_space=pl.ANY),
            pl.BlockSpec(memory_space=pl.ANY),
        ],
        out_specs=pl.BlockSpec(memory_space=pltpu.VMEM),
        scratch_shapes=[
            pltpu.VMEM((SLOTS + 1, TILE, TILE), jnp.bfloat16),
            pltpu.VMEM((PASSES, 256, DEPTH), jnp.bfloat16),
            pltpu.VMEM((UNITS, 128, COLS), F32),
            *messages,
            *messages,
            pltpu.VMEM((48, 4096), jnp.bfloat16),
            pltpu.SemaphoreType.DMA((PARTS,)),
            pltpu.SemaphoreType.DMA((2 * PASSES,)),
            pltpu.SemaphoreType.DMA((PASSES, 8)),
            pltpu.SemaphoreType.DMA((PASSES, 8)),
            pltpu.SemaphoreType.DMA((UNITS, 5)),
            pltpu.SemaphoreType.DMA((UNITS, 5)),
        ],
        compiler_params=pltpu.CompilerParams(
            collective_id=0, has_side_effects=True, vmem_limit_bytes=56 << 20
        ),
        name="ladder",
    )(inverse.astype(jnp.int32), pair_amps, integrals[0, 0])


def solution(mesh):
    placed = (
        P("vrow", "vcol"),
        P("vrow", "vcol", None, None, None),
        P("vrow", "vcol", None),
        P("vrow", "vcol"),
    )
    return jax.shard_map(
        per_device, mesh=mesh, in_specs=placed, out_specs=P("vcol", "vrow"), check_vma=False
    )
```

```python
import jax
import jax.numpy as jnp
from jax import lax
from jax.experimental import pallas as pl
from jax.experimental.pallas import tpu as pltpu
from jax.sharding import PartitionSpec as P

MESH = pl.DeviceIdType.MESH
F32 = jnp.float32
TILE = 128
SLOTS = 512
CD = 16
DEPTH = CD * TILE
PASSES = 3
COLS = 1024
UNITS = 12
PER_PASS = 4
DIRECT = 3
LAGS = (2, 4, 6)
LEVELS = 32766.0
PARTS = 16


def kernel(
    index, count, amps, w_hbm, out, inv_v, inv, wv, a, d, acc, sent1, got1, sent2, got2, held,
    isem, wsem, asem, gsend, grecv, ssend, srecv,
):
    vrow, vcol = lax.axis_index("vrow"), lax.axis_index("vcol")
    z, core = vrow // 2, vrow % 2
    x, y = vcol // 4, vcol % 4

    per = SLOTS // PARTS

    def load_part(c):
        part, into = pl.ds(c * per, per), pl.ds(1 + c * per, per)
        return pltpu.make_async_copy(w_hbm.at[part], wv.at[into], wsem.at[c])

    def load_rows(s, i):
        return pltpu.make_async_copy(
            amps.at[pl.ds(48 * i + 16 * s, 16)],
            a.at[s, pl.ds(32 * vrow + 16 * i, 16)],
            asem.at[2 * s + i],
        )

    for s in range(PASSES):
        for i in range(2):
            load_rows(s, i).start()

    above, below, across = (vrow + 2) % 8, (vrow + 6) % 8, (vrow + 4) % 8
    sibling = 2 * z + 1 - core
    along_x = [((x + n) % 4) * 4 + y for n in range(4)]
    along_y = [x * 4 + (y + n) % 4 for n in range(4)]

    barrier = pltpu.get_barrier_semaphore()
    peers = [(above, vcol), (below, vcol), (across, vcol), (sibling, vcol)]
    peers += [(vrow, p) for p in along_x[1:] + along_y[1:]]
    for peer in peers:
        pl.semaphore_signal(barrier, inc=1, device_id=peer, device_id_type=MESH)
    wv[0] = jnp.zeros((TILE, TILE), jnp.bfloat16)
    for s in range(PASSES):
        for i in range(2):
            load_rows(s, i).wait()
    pl.semaphore_wait(barrier, len(peers))

    own = 32 * vrow
    from_rows = [own, 32 * below, 32 * above, 32 * across]
    near_rows = [32 * ((sibling + n) % 8) for n in (0, 6, 2, 4)]

    def piece(s, first, target, kind, rows=32):
        ref = a.at[s, pl.ds(pl.multiple_of(first, 16), rows)]
        return pltpu.make_async_remote_copy(
            src_ref=ref, dst_ref=ref,
            send_sem=gsend.at[s, kind], recv_sem=grecv.at[s, kind],
            device_id=(target, vcol), device_id_type=MESH,
        )

    def gather_start(s):
        piece(s, own, above, 1).start()
        piece(s, own, below, 2).start()
        piece(s, own, sibling, 4).start()

    def gather_near(s):
        piece(s, from_rows[1], sibling, 1).wait_recv()
        piece(s, from_rows[1], above, 0, 16).start()
        piece(s, from_rows[1], sibling, 5).start()
        piece(s, from_rows[2], sibling, 2).wait_recv()
        piece(s, from_rows[2] + 16, below, 3, 16).start()
        piece(s, from_rows[2], sibling, 6).start()

    def gather_far(s):
        piece(s, from_rows[3], sibling, 0, 16).wait_recv()
        piece(s, from_rows[3] + 16, sibling, 3, 16).wait_recv()
        piece(s, from_rows[3], sibling, 7).start()

    def gather_end(s):
        for n in range(4):
            piece(s, near_rows[n], sibling, 4 + n).wait_recv()

    def gather_sent(s):
        for n in range(8):
            piece(s, own, sibling, n, 16 if n in (0, 3) else 32).wait_send()

    def message1(u, n, kind, slot=None, rows=272):
        target = (along_x if kind == "x" else along_y)[n]
        slot = n - 1 if slot is None else slot
        part = pl.ds(0, rows)
        return pltpu.make_async_remote_copy(
            src_ref=sent1.at[u, slot, part], dst_ref=got1.at[u, slot, part],
            send_sem=ssend.at[u, slot], recv_sem=srecv.at[u, slot],
            device_id=(vrow, target), device_id_type=MESH,
        )

    def passed_on(u, n, kind):
        return message1(u, n, kind, n, 144)

    def message2(u, n, kind):
        rows = pl.ds(0, 80 if kind == "x" else 144)
        target = (along_y if kind == "x" else along_x)[n]
        slot = 0 if kind == "y" and n == 3 else n - 1
        return pltpu.make_async_remote_copy(
            src_ref=sent2.at[u, slot, rows], dst_ref=got2.at[u, n - 1, rows],
            send_sem=ssend.at[u, 3 + n], recv_sem=srecv.at[u, 3 + n],
            device_id=(vrow, target), device_id_type=MESH,
        )

    def pack(ref, values):
        most = jnp.abs(values[0])
        for value in values[1:]:
            most = jnp.maximum(most, jnp.abs(value))
        most = jnp.maximum(jnp.max(most, axis=0, keepdims=True), 1e-30)
        code = jnp.ceil(jnp.log(most) * 256.0)
        factor = jnp.exp(code * (-1.0 / 256.0)) * LEVELS
        for n, value in enumerate(values):
            q = jnp.round(value * factor).astype(jnp.int32)
            ref[16 * n : 16 * n + 16] = q.astype(jnp.int16)
        n = len(values)
        wide = jnp.broadcast_to(code, (16, TILE)).astype(jnp.int32)
        ref[16 * n : 16 * n + 16] = wide.astype(jnp.int16)

    def unpacked(ref, count):
        code = ref[16 * count : 16 * count + 16].astype(jnp.int32).astype(F32)
        factor = jnp.exp(code * (1.0 / 256.0)) * (1.0 / LEVELS)

        def at(n):
            return ref[16 * n : 16 * n + 16].astype(jnp.int32).astype(F32) * factor

        return at

    def region(u, kind, to):
        pieces = []
        if kind == "x":
            for c in range(4):
                col = pl.multiple_of(512 * (to // 2) + TILE * c, TILE)
                for g in range(4):
                    row = pl.multiple_of(64 * (to % 2) + 16 * g, 16)
                    pieces.append(d.at[u, pl.ds(row, 16), pl.ds(col, TILE)])
        else:
            for half in range(2):
                row = pl.multiple_of(64 * half + 16 * to, 16)
                for c in range(8):
                    pieces.append(d.at[u, pl.ds(row, 16), pl.ds(TILE * c, TILE)])
        return pieces

    def multiply(u):
        s, j = u // PER_PASS, u % PER_PASS

        right = []
        for t in range(COLS // TILE):
            right.append(jnp.concatenate([wv[inv[j, t * CD + k]] for k in range(CD)], 0))
        right = jnp.concatenate(right, 1)
        both = jnp.dot(a[s], right, preferred_element_type=F32)
        d[u] = both[:128] - both[128:]

    def first(u, kind):
        me = x if kind == "x" else y
        for n in (2, 1, 3):
            pieces = region(u, kind, (me + n) % 4)
            pack(sent1.at[u, n - 1], [p[...] for p in pieces])
            message1(u, n, kind).start()

    def first_ring(u, kind):
        me = x if kind == "x" else y
        far = region(u, kind, (me + 2) % 4)
        right, left = region(u, kind, (me + 1) % 4), region(u, kind, (me + 3) % 4)
        pack(sent1.at[u, 0], [p[...] for p in far[:8] + right[8:]])
        message1(u, 1, kind).start()
        pack(sent1.at[u, 2], [p[...] for p in far[8:] + left[:8]])
        message1(u, 3, kind).start()

    def relay(u, kind):
        me = x if kind == "x" else y
        message1(u, 1, kind).wait_recv()
        got = unpacked(got1.at[u, 0], 16)
        right = region(u, kind, (me + 1) % 4)[:8]
        pack(sent1.at[u, 1], [p[...] + got(n) for n, p in enumerate(right)])
        passed_on(u, 1, kind).start()
        message1(u, 3, kind).wait_recv()
        got = unpacked(got1.at[u, 2], 16)
        left = region(u, kind, (me + 3) % 4)[8:]
        pack(sent1.at[u, 3], [p[...] + got(n) for n, p in enumerate(left)])
        passed_on(u, 3, kind).start()

    def second_ring(u, kind):
        passed_on(u, 1, kind).wait_recv()
        passed_on(u, 3, kind).wait_recv()
        plain = [unpacked(got1.at[u, 2], 16), unpacked(got1.at[u, 0], 16)]
        summed = [unpacked(got1.at[u, 1], 8), unpacked(got1.at[u, 3], 8)]
        for n, ref in enumerate(region(u, kind, x if kind == "x" else y)):
            h = n // 8
            acc[u, 16 * n : 16 * n + 16] = ref[...] + plain[h](n % 8 + 8) + summed[h](n % 8)
        send_second(u, kind)

    def second(u, kind):
        for n in (1, 3, 2):
            message1(u, n, kind).wait_recv()
        got = [unpacked(got1.at[u, n], 16) for n in range(3)]
        for n, ref in enumerate(region(u, kind, x if kind == "x" else y)):
            acc[u, 16 * n : 16 * n + 16] = ref[...] + (got[0](n) + got[1](n)) + got[2](n)
        send_second(u, kind)

    def send_second(u, kind):
        if kind == "x":
            for n in (2, 1, 3):
                row = 16 * ((y + n) % 4)
                values = []
                for c in range(4):
                    values.append(acc[u, pl.ds(pl.multiple_of(64 * c + row, 16), 16)])
                pack(sent2.at[u, n - 1], values)
                message2(u, n, kind).start()
        else:
            for n in (2, 1):
                row = 128 * ((x + n) % 2)
                values = []
                for c in range(8):
                    values.append(acc[u, pl.ds(pl.multiple_of(row + 16 * c, 16), 16)])
                pack(sent2.at[u, n - 1], values)
                message2(u, n, kind).start()
                if n == 1:
                    message2(u, 3, kind).start()

    def held_ref(u, first_col, cols):
        s, j = u // PER_PASS, u % PER_PASS
        col = pl.multiple_of(COLS * j + first_col, TILE)
        return held.at[pl.ds(pl.multiple_of(16 * s, 16), 16), pl.ds(col, cols)]

    def third(u, kind):
        for n in (1, 3, 2):
            message2(u, n, kind).wait_recv()
        count = 4 if kind == "x" else 8
        got = [unpacked(got2.at[u, n], count) for n in range(3)]
        for c in range(count):
            if kind == "x":
                row, col = 64 * c + 16 * y, 512 * (x // 2) + TILE * c
            else:
                row, col = 128 * (x % 2) + 16 * c, TILE * c
            mine = acc[u, pl.ds(pl.multiple_of(row, 16), 16)]
            total = mine + (got[0](c) + got[1](c)) + got[2](c)
            held_ref(u, col, TILE)[...] = total.astype(jnp.bfloat16)
        if kind == "x":
            deliver(u, x // 2).start()

    def deliver(u, half):
        ref = held_ref(u, 512 * half, 512)
        return pltpu.make_async_remote_copy(
            src_ref=ref, dst_ref=ref,
            send_sem=ssend.at[u, 7], recv_sem=srecv.at[u, 7],
            device_id=(vrow, along_x[2]), device_id_type=MESH,
        )

    gather_start(0)
    for c in range(PARTS):
        load_part(c).start()
    slots = lax.broadcasted_iota(jnp.int32, (TILE, TILE), 0)
    pairs = lax.broadcasted_iota(jnp.int32, (TILE, TILE), 1)
    live = count[0, 0]
    for g in range(4):
        found = jnp.zeros((1, TILE), jnp.int32)
        for q in range(4):
            row = jnp.broadcast_to(index[q : q + 1], (TILE, TILE))
            hit = (jnp.transpose(row) == pairs + TILE * g) & (slots < live - TILE * q)
            most = jnp.max(jnp.where(hit, slots + (TILE * q + 1), 0), axis=0, keepdims=True)
            found = jnp.maximum(found, most)
        inv_v[g : g + 1] = found
    to_scalar = pltpu.make_async_copy(inv_v, inv, isem)
    to_scalar.start()
    gather_near(0)
    gather_start(1)
    gather_far(0)
    gather_end(0)
    to_scalar.wait()
    for c in range(PARTS):
        load_part(c).wait()

    ring = UNITS - DIRECT

    def of_kind(u, step):
        @pl.when(u % 3 == 1)
        def _():
            step(u, "x")

        @pl.when(u % 3 != 1)
        def _():
            step(u, "y")

    def sends_done(u, kind):
        for n in (1, 3):
            message1(u, n, kind).wait_send()

        @pl.when(u < ring)
        def _():
            for n in (1, 3):
                passed_on(u, n, kind).wait_send()

        @pl.when(u >= ring)
        def _():
            message1(u, 2, kind).wait_send()

    def turn(t, unused):
        @pl.when(t < UNITS)
        def _():
            s, step = t // PER_PASS, t % PER_PASS

            @pl.when((step == 0) & (s > 0))
            def _():
                gather_end(s)

            multiply(t)

            @pl.when(t < ring)
            def _():
                of_kind(t, first_ring)

            @pl.when(t >= ring)
            def _():
                of_kind(t, first)

        @pl.when(t == 0)
        def _():
            gather_near(1)
            gather_start(2)

        @pl.when(t == 2)
        def _():
            gather_far(1)

        @pl.when(t == 3)
        def _():
            gather_near(2)

        @pl.when(t == 5)
        def _():
            gather_far(2)

        u = t - LAGS[0]

        @pl.when((u >= 0) & (u < ring))
        def _():
            of_kind(u, relay)

        @pl.when((u >= ring) & (u < UNITS))
        def _():
            of_kind(u, second)

        u = t - LAGS[1]

        @pl.when((u >= 0) & (u < ring))
        def _():
            of_kind(u, second_ring)

        @pl.when((u >= ring) & (u < UNITS))
        def _():
            of_kind(u, third)

        u = t - LAGS[2]

        @pl.when((u >= 0) & (u < ring))
        def _():
            of_kind(u, third)

        @pl.when(u >= 0)
        def _():
            of_kind(u, sends_done)

        return unused

    turns = max(UNITS + LAGS[1], ring + LAGS[2])
    lax.fori_loop(0, turns, turn, 0)

    for u in range(turns - LAGS[2], UNITS):
        sends_done(u, "x" if u % 3 == 1 else "y")

    def finish(u, unused):
        def sent(u, kind):
            for n in (1, 2, 3):
                message2(u, n, kind).wait_send()
            if kind == "x":
                deliver(u, x // 2).wait_send()
                deliver(u, 1 - x // 2).wait_recv()

        of_kind(u, sent)
        return unused

    lax.fori_loop(0, UNITS, finish, 0)
    for s in range(PASSES):
        gather_sent(s)

    sign = (1 - 2 * (x // 2)).astype(jnp.bfloat16)
    out[...] = held[...] * sign


def per_device(pair_amps, integrals, block_index, block_count):
    first_phase = pltpu.VMEM((UNITS, 4, 272, TILE), jnp.int16)
    second_phase = pltpu.VMEM((UNITS, 3, 144, TILE), jnp.int16)
    return pl.pallas_call(
        kernel,
        out_shape=jax.ShapeDtypeStruct((48, 4096), jnp.bfloat16),
        in_specs=[
            pl.BlockSpec(memory_space=pltpu.VMEM),
            pl.BlockSpec(memory_space=pltpu.SMEM),
            pl.BlockSpec(memory_space=pl.ANY),
            pl.BlockSpec(memory_space=pl.ANY),
        ],
        out_specs=pl.BlockSpec(memory_space=pltpu.VMEM),
        scratch_shapes=[
            pltpu.VMEM((4, TILE), jnp.int32),
            pltpu.SMEM((4, TILE), jnp.int32),
            pltpu.VMEM((SLOTS + 1, TILE, TILE), jnp.bfloat16),
            pltpu.VMEM((PASSES, 256, DEPTH), jnp.bfloat16),
            pltpu.VMEM((UNITS, 128, COLS), F32),
            pltpu.VMEM((UNITS, 256, TILE), F32),
            first_phase,
            first_phase,
            second_phase,
            second_phase,
            pltpu.VMEM((48, 4096), jnp.bfloat16),
            pltpu.SemaphoreType.DMA,
            pltpu.SemaphoreType.DMA((PARTS,)),
            pltpu.SemaphoreType.DMA((2 * PASSES,)),
            pltpu.SemaphoreType.DMA((PASSES, 8)),
            pltpu.SemaphoreType.DMA((PASSES, 8)),
            pltpu.SemaphoreType.DMA((UNITS, 8)),
            pltpu.SemaphoreType.DMA((UNITS, 8)),
        ],
        compiler_params=pltpu.CompilerParams(
            collective_id=0, has_side_effects=True, vmem_limit_bytes=56 << 20
        ),
        name="ladder",
    )(block_index.reshape(4, TILE), block_count, pair_amps, integrals[0, 0])


def solution(mesh):
    placed = (
        P("vrow", "vcol"),
        P("vrow", "vcol", None, None, None),
        P("vrow", "vcol", None),
        P("vrow", "vcol"),
    )
    return jax.shard_map(
        per_device, mesh=mesh, in_specs=placed, out_specs=P("vcol", "vrow"), check_vma=False
    )
```
